32 devices in a mesh: grp: 2 (over x), seq: 8 (over z, y), ch: 2 (over core).
Axes of the slice: x: 2, y: 2, z: 4, core: 2. Of those that a mesh axis runs over, the one named last changes fastest.
Arguments:
- q_proj: float32 [2048, 2048], P(('grp', 'seq'), 'ch'), parts along dimension 0, may hold values from -6 to 6
- k_proj: float32 [2048, 2048], P(('grp', 'seq'), 'ch'), parts along dimension 0, may hold values from -6 to 6
- v_proj: float32 [2048, 2048], P(('grp', 'seq'), 'ch'), parts along dimension 0, may hold values from -6 to 6
- short_taps: float32 [3, 3, 2048], P(None, None, 'ch'), may hold values from -3 to 3
- frequencies: int32 [16], replicated, may hold values from 1 to 511
- w_first: float32 [33, 64], replicated, may hold values from -1 to 1
- b_first: float32 [64], replicated, may hold values from -3.140625 to 3.140625
- w_second: float32 [64, 64], replicated, may hold values from -0.75 to 0.75
- b_second: float32 [64], replicated, may hold values from -3.140625 to 3.140625
- w_last: float32 [64, 2048], P(None, 'ch'), may hold values from -0.75 to 0.75
- rates: float32 [2048], P('ch'), may hold values from 0.5 to 200
- skip: float32 [2048], P('ch'), may hold values from -4 to 4
Outputs:
- gated: float32 [2048, 2048], P(('grp', 'seq'), 'ch'), parts along dimension 0
The draws below stay inside these ranges and needn't reach their ends.
There are 2 independent parts, one for each index of `grp`. The reference program is written for one: setup_inputs(seed, part) draws one part's arguments, and reference() takes and returns one part's arrays. A program takes and returns all parts, laid end to end along the dimension named above; an argument that names none is the same for every part. Nothing has to cross between parts.
All inputs are finite; a program needn't handle non-finite values.
Results may differ from the reference program's by a relative error of at most 0.0003.
Values sent between devices are 32-bit elements; how exact they have to be, the bound alone decides.
A program may use at most 64 MiB of HBM per device.

```python
import math
import jax
import jax.numpy as jnp
from jax import lax

W = 2048
ORDER = 64
BANDS = 16
EMB = 33
SEQ_LEN = 1024


def touch_ends(array, own_key, smallest, largest):
    dims = array.shape
    index_at = [jax.random.randint(jax.random.fold_in(own_key, axis), (), 0, dims[axis]) for axis in range(len(dims))]
    array = array.at[tuple(index_at)].set(smallest)
    longest = dims.index(max(dims))
    index_at[longest] = (index_at[longest] + 1) % dims[longest]
    return array.at[tuple(index_at)].set(largest)


def shard_levels(stream_key, dims, pieces, least, largest):
    loudness = 1.0
    for axis_at, parts in pieces:
        heights = jax.random.uniform(jax.random.fold_in(jax.random.fold_in(stream_key, 6), axis_at), (parts,), jnp.float32, least / len(pieces), largest / len(pieces))
        loudness = loudness * jnp.repeat(jnp.exp(heights), dims[axis_at] // parts).reshape((-1,) + (1,) * (len(dims) - 1 - axis_at))
    return loudness


def centred(stream_key, dims, deviation, most, cuts=(), kind=jnp.bfloat16):
    factor_of = shard_levels(stream_key, dims, cuts, -0.22, 0.18) if cuts else 1.0
    entries = jax.random.normal(stream_key, dims, jnp.float32) * deviation * factor_of
    return jnp.minimum(jnp.maximum(entries, -most), most).astype(kind)


def setup_inputs(seed: int = 0, part: int = 0) -> dict:
    streams_of = jax.random.split(jax.random.key(seed), 13)
    part_splits = jax.random.split(jax.random.fold_in(streams_of[12], part), 13)
    q_proj = centred(part_splits[0], (SEQ_LEN, W), 1.0, 6.0, ((0, 8), (1, 2)), jnp.float32)
    k_proj = centred(part_splits[1], (SEQ_LEN, W), 1.0, 6.0, ((0, 8), (1, 2)), jnp.float32)
    v_proj = centred(part_splits[2], (SEQ_LEN, W), 1.0, 6.0, ((0, 8), (1, 2)), jnp.float32)
    short_taps = centred(streams_of[3], (3, 3, W), 0.6, 3.0, ((2, 2),), jnp.float32)
    frequencies = touch_ends(jax.random.randint(streams_of[4], (BANDS,), 1, min(SEQ_LEN // 2, 8192)), jax.random.fold_in(streams_of[4], 1), 1, (min(SEQ_LEN // 2, 8192)) - 1).astype(jnp.int32)
    w_first = centred(streams_of[5], (EMB, ORDER), EMB ** -0.5, 1.0, (), jnp.float32)
    b_first = jnp.clip(jax.random.uniform(streams_of[6], (ORDER,), jnp.float32, -3.140625, 3.140625), -3.140625, 3.140625)
    w_second = centred(streams_of[7], (ORDER, ORDER), ORDER ** -0.5, 0.75, (), jnp.float32)
    b_second = jnp.clip(jax.random.uniform(streams_of[8], (ORDER,), jnp.float32, -3.140625, 3.140625), -3.140625, 3.140625)
    w_last = centred(streams_of[9], (ORDER, W), ORDER ** -0.5, 0.75, ((1, 2),), jnp.float32)
    rates = jnp.clip(jnp.exp(math.log(200.0) - 5.9914645 * jax.random.uniform(streams_of[10], (W,), jnp.float32) ** shard_levels(streams_of[10], (W,), ((0, 2),), -0.2, 0.2)), 0.5, 200.0)
    skip = centred(streams_of[11], (W,), 1.0, 4.0, ((0, 2),), jnp.float32)
    return dict(q_proj=q_proj, k_proj=k_proj, v_proj=v_proj, short_taps=short_taps, frequencies=frequencies, w_first=w_first, b_first=b_first, w_second=w_second, b_second=b_second, w_last=w_last, rates=rates, skip=skip)


HIGH = lax.Precision.HIGHEST
EPS = 1e-06
DECAY_FLOOR = 0.05

def causal_short(values, tail, taps):
    count = values.shape[0]
    padded = jnp.concatenate([tail, values], axis=0)
    return taps[0] * values + taps[1] * padded[1:count + 1] + taps[2] * padded[0:count]

def filter_rows(positions, length, frequencies, w_first, b_first, w_second, b_second, w_last, rates):
    product = positions[:, None] * frequencies[None, :] % length
    angle = 2.0 * math.pi / length * product.astype(jnp.float32)
    place = positions.astype(jnp.float32) / length
    features = jnp.concatenate([place[:, None], jnp.cos(angle), jnp.sin(angle)], axis=1)
    hidden = jnp.sin(jnp.dot(features, w_first, precision=HIGH) + b_first)
    hidden = jnp.sin(jnp.dot(hidden, w_second, precision=HIGH) + b_second)
    raw = jnp.dot(hidden, w_last, precision=HIGH)
    return raw * (jnp.exp(-place[:, None] * rates[None, :]) + DECAY_FLOOR)

def reference(q_proj, k_proj, v_proj, short_taps, frequencies, w_first, b_first, w_second, b_second, w_last, rates, skip):
    length = q_proj.shape[0]
    tail = jnp.zeros((2, q_proj.shape[1]), jnp.float32)
    q_short = causal_short(q_proj, tail, short_taps[0])
    k_short = causal_short(k_proj, tail, short_taps[1])
    v_short = causal_short(v_proj, tail, short_taps[2])
    mixed = k_short * v_short
    positions = jnp.arange(length, dtype=jnp.int32)
    filt = filter_rows(positions, length, frequencies, w_first, b_first, w_second, b_second, w_last, rates)
    energy = lax.optimization_barrier(jnp.sum(filt * filt, axis=0))
    unit = filt / jnp.sqrt(energy + EPS)
    spectrum = jnp.fft.rfft(mixed, n=2 * length, axis=0) * jnp.fft.rfft(unit, n=2 * length, axis=0)
    conv = jnp.fft.irfft(spectrum, n=2 * length, axis=0)[:length]
    return q_short * (conv + skip * mixed)
```

```python
import functools
import math

import jax
import jax.numpy as jnp
import numpy as np
from jax import lax
from jax.experimental import pallas as pl
from jax.experimental.pallas import tpu as pltpu
from jax.sharding import PartitionSpec as P

HIGH = lax.Precision.HIGHEST
EPS = 1e-06
DECAY_FLOOR = 0.05
LANES = 128
EDGE = 8


def transform_tables(block):
    freq = 2 * np.arange(block)[:, None] + 1
    place = np.arange(2 * block)[None, :]
    angle = 2.0 * np.pi / (4 * block) * (freq * place % (4 * block))
    forward = np.concatenate([np.cos(angle), -np.sin(angle)], axis=0)
    late = angle[:, block:].T
    inverse = np.concatenate([np.cos(late), -np.sin(late)], axis=1) / block
    return forward.astype(np.float32), inverse.astype(np.float32)


def small_sine(x):
    turns = jnp.floor(x * (1.0 / math.pi) + 0.5)
    rest = x - turns * 3.140625
    rest = rest - turns * 9.67502593994140625e-4
    rest = rest - turns * 1.509957990978376432e-7
    odd = (turns.astype(jnp.int32) & 1) == 1
    rest = jnp.where(odd, -rest, rest)
    square = rest * rest
    poly = 2.6083159809786593541503e-06
    poly = poly * square - 0.0001981069071916863322258
    poly = poly * square + 0.00833307858556509017944336
    poly = poly * square - 0.166666597127914428710938
    return rest + rest * (square * poly)


def contract_rows(left, right):
    return lax.dot_general(
        left, right, (((0,), (0,)), ((), ())), precision=HIGH,
        preferred_element_type=jnp.float32,
    )


def kernel(
    parts, flat,
    q_ref, k_ref, v_ref, taps_ref, freq_ref, w1_ref, b1_ref, w2_ref, b2_ref,
    w3_ref, rates_ref, skip_ref, fwd_ref, inv_ref,
    out_ref,
    tails, send, recv, back, conv, feat, w1x, hid, w2x, filt, gain, spec, prod,
    tail_sems, main_sems, edge_sems, back_sems,
):
    tokens, cw = send.shape[1], send.shape[2]
    length = tokens * parts
    me = lax.axis_index("seq")
    order = sorted(range(1, parts), key=lambda s: (-min(s, parts - s), s))

    def ahead(s):
        return lax.rem(me + s, parts)

    def behind(s):
        return lax.rem(me + parts - s, parts)

    def cols(ref, d, rows=slice(None)):
        if flat:
            return ref[rows, pl.ds(pl.multiple_of(d * cw, LANES), cw)]
        return ref[d, rows, :]

    def remote(src, dst, sems, s, dest):
        return pltpu.make_async_remote_copy(
            src_ref=src, dst_ref=dst, send_sem=sems.at[0, s], recv_sem=sems.at[1, s],
            device_id={"seq": dest}, device_id_type=pl.DeviceIdType.MESH,
        )

    barrier = pltpu.get_barrier_semaphore()
    for s in order:
        pl.semaphore_signal(
            barrier, inc=1, device_id={"seq": ahead(s)},
            device_id_type=pl.DeviceIdType.MESH,
        )
    pl.semaphore_wait(barrier, parts - 1)

    last = pl.ds(tokens - EDGE, EDGE)
    tail_copies = []
    for j, ref in enumerate((k_ref, v_ref, q_ref)):
        src = ref.at[last, :] if flat else ref.at[:, last, :]
        copy = remote(src, tails.at[j], tail_sems, j, ahead(1))
        copy.start()
        tail_copies.append(copy)

    def short(ref, j, d):
        rows = tokens - EDGE
        x = cols(ref, d)
        taps = cols(taps_ref, d)
        return (
            taps[3 * j : 3 * j + 1] * x[EDGE:]
            + taps[3 * j + 1 : 3 * j + 2] * x[EDGE - 1 : tokens - 1]
            + taps[3 * j + 2 : 3 * j + 3] * x[EDGE - 2 : tokens - 2]
        )

    def short_edge(ref, j, slot, d):
        x = cols(ref, d, slice(0, EDGE))
        before = cols(tails.at[slot], d)
        before = jnp.where(me == 0, jnp.zeros_like(before), before)
        both = jnp.concatenate([before, x], axis=0)
        taps = cols(taps_ref, d)
        return (
            taps[3 * j : 3 * j + 1] * x
            + taps[3 * j + 1 : 3 * j + 2] * both[EDGE - 1 : 2 * EDGE - 1]
            + taps[3 * j + 2 : 3 * j + 3] * both[EDGE - 2 : 2 * EDGE - 2]
        )

    main_rows = pl.ds(EDGE, tokens - EDGE)
    edge_rows = pl.ds(0, EDGE)
    main_copies, edge_copies, back_copies = {}, {}, {}
    for s in order + [0]:
        d = ahead(s)
        send[d, EDGE:, :] = short(k_ref, 1, d) * short(v_ref, 2, d)
        if s:
            copy = remote(
                send.at[d, main_rows, :], recv.at[me, main_rows, :], main_sems, s, d
            )
            copy.start()
            main_copies[s] = copy
    for copy in tail_copies:
        copy.wait()
    for s in order + [0]:
        d = ahead(s)
        send[d, :EDGE, :] = short_edge(k_ref, 1, 0, d) * short_edge(v_ref, 2, 1, d)
        if s:
            copy = remote(
                send.at[d, edge_rows, :], recv.at[me, edge_rows, :], edge_sems, s, d
            )
            copy.start()
            edge_copies[s] = copy

    width = feat.shape[1]
    bands = freq_ref.shape[0]
    row = lax.broadcasted_iota(jnp.int32, (2 * bands, width), 0)
    position = lax.broadcasted_iota(jnp.int32, (2 * bands, width), 1)
    cycles = jnp.zeros((2 * bands, width), jnp.int32)
    for b in range(bands):
        cycles = jnp.where((row == b) | (row == b + bands), freq_ref[b], cycles)
    quarter = jnp.where(row < bands, length // 4, 0)
    phase = (position * cycles + quarter) & (length - 1)
    feat[...] = jnp.zeros_like(feat)
    feat[0 : 2 * bands, :] = small_sine((2.0 * math.pi / length) * phase.astype(jnp.float32))
    feat[2 * bands : 2 * bands + 1, :] = position[0:1].astype(jnp.float32) / length
    feat[2 * bands + 1 : 2 * bands + 2, :] = jnp.ones((1, width), jnp.float32)
    w1x[...] = jnp.zeros_like(w1x)
    w1x[0 : 2 * bands, :] = w1_ref[1 : 2 * bands + 1, :]
    w1x[2 * bands : 2 * bands + 1, :] = w1_ref[0:1, :]
    w1x[2 * bands + 1 : 2 * bands + 2, :] = b1_ref[...]
    hidden_units = w2_ref.shape[0]
    hid[...] = jnp.zeros_like(hid)
    hid[hidden_units : hidden_units + 1, :] = jnp.ones((1, width), jnp.float32)
    hid[0:hidden_units, :] = small_sine(contract_rows(w1x[...], feat[...]))
    w2x[...] = jnp.zeros_like(w2x)
    w2x[0:hidden_units, :] = w2_ref[...]
    w2x[hidden_units : hidden_units + 1, :] = b2_ref[...]
    hid[0:hidden_units, :] = small_sine(contract_rows(w2x[...], hid[...]))

    filt[0:tokens, :] = jnp.zeros((tokens, cw), jnp.float32)
    w_last = cols(w3_ref, me)
    rates = cols(rates_ref, me)

    def filter_block(j, energy):
        start = pl.multiple_of(j * tokens, tokens)
        raw = contract_rows(hid[0:hidden_units, pl.ds(start, tokens)], w_last)
        n = lax.broadcasted_iota(jnp.int32, (tokens, cw), 0) + j * tokens
        place = n.astype(jnp.float32) / length
        values = raw * (jnp.exp(-place * rates) + DECAY_FLOOR)
        filt[pl.ds(pl.multiple_of(start + tokens, tokens), tokens), :] = values
        return energy + jnp.sum(values * values, axis=0, keepdims=True)

    energy = lax.fori_loop(0, parts, filter_block, jnp.zeros((1, cw), jnp.float32))
    scale = 1.0 / jnp.sqrt(energy + EPS)

    @pl.loop(0, parts)
    def _(j):
        window = filt[pl.ds(pl.multiple_of(j * tokens, tokens), 2 * tokens), :]
        gain[j] = scale * jnp.dot(
            fwd_ref[...], window, precision=HIGH, preferred_element_type=jnp.float32
        )
        prod[j] = jnp.zeros((2 * tokens, cw), jnp.float32)

    def absorb(block, i):
        spec[...] = jnp.dot(
            fwd_ref[:, 0:tokens], block, precision=HIGH, preferred_element_type=jnp.float32
        )

        @pl.loop(0, parts - i)
        def _(j):
            x_re, x_im = spec[0:tokens, :], spec[tokens:, :]
            g_re, g_im = gain[j, 0:tokens, :], gain[j, tokens:, :]
            prod[i + j, 0:tokens, :] += x_re * g_re - x_im * g_im
            prod[i + j, tokens:, :] += x_re * g_im + x_im * g_re

    absorb(send[me], me)
    for s in order:
        main_copies[s].wait_recv()
        edge_copies[s].wait_recv()
        absorb(recv[behind(s)], behind(s))

    def restore(m):
        return jnp.dot(
            inv_ref[...], prod[m], precision=HIGH, preferred_element_type=jnp.float32
        )

    for s in order:
        m = ahead(s)
        conv[m] = restore(m)
        copy = remote(conv.at[m], back.at[me], back_sems, s, m)
        copy.start()
        back_copies[s] = copy
    conv[me] = restore(me)

    def gate(result, d):
        q_short = jnp.concatenate(
            [short_edge(q_ref, 0, 2, d), short(q_ref, 0, d)], axis=0
        )
        value = q_short * (result + cols(skip_ref, d) * send[d])
        if flat:
            out_ref[:, pl.ds(pl.multiple_of(d * cw, LANES), cw)] = value
        else:
            out_ref[d] = value

    gate(conv[me], me)
    for s in order:
        back_copies[s].wait_recv()
        gate(back[behind(s)], behind(s))
    for s in order:
        main_copies[s].wait_send()
        edge_copies[s].wait_send()
        back_copies[s].wait_send()


def local(
    q_proj, k_proj, v_proj, short_taps, frequencies, w_first, b_first, w_second,
    b_second, w_last, rates, skip,
):
    tokens, width = q_proj.shape
    parts = lax.axis_size("seq")
    cw = width // parts
    flat = cw % LANES == 0
    length = tokens * parts
    order = w_second.shape[0]
    features = w_first.shape[0]

    def split(array):
        if flat:
            return array
        return array.reshape(array.shape[0], parts, cw).transpose(1, 0, 2)

    forward, inverse = transform_tables(tokens)
    tail_shape = (3, EDGE, width) if flat else (3, parts, EDGE, cw)
    out_shape = (tokens, width) if flat else (parts, tokens, cw)
    f32 = jnp.float32
    feature_rows = (features + 1 + 7) // 8 * 8
    blocks = pltpu.VMEM((parts, tokens, cw), f32)
    spectra = pltpu.VMEM((parts, 2 * tokens, cw), f32)
    vmem = pl.BlockSpec(memory_space=pltpu.VMEM)
    smem = pl.BlockSpec(memory_space=pltpu.SMEM)
    sems = pltpu.SemaphoreType.DMA((2, parts))
    out = pl.pallas_call(
        functools.partial(kernel, parts, flat),
        out_shape=jax.ShapeDtypeStruct(out_shape, f32),
        in_specs=[vmem] * 4 + [smem] + [vmem] * 9,
        out_specs=vmem,
        scratch_shapes=[
            pltpu.VMEM(tail_shape, f32),
            blocks, blocks, blocks, blocks,
            pltpu.VMEM((feature_rows, length), f32),
            pltpu.VMEM((feature_rows, order), f32),
            pltpu.VMEM((order + 8, length), f32),
            pltpu.VMEM((order + 8, order), f32),
            pltpu.VMEM((length + tokens, cw), f32),
            spectra,
            pltpu.VMEM((2 * tokens, cw), f32),
            spectra,
            pltpu.SemaphoreType.DMA((2, 3)),
            sems, sems, sems,
        ],
        compiler_params=pltpu.CompilerParams(
            collective_id=0, has_side_effects=True, vmem_limit_bytes=48 * 1024 * 1024
        ),
        cost_estimate=pl.CostEstimate(
            flops=6 * length * tokens * cw * 8, bytes_accessed=16 * tokens * width,
            transcendentals=length * cw,
        ),
    )(
        split(q_proj), split(k_proj), split(v_proj),
        split(short_taps.reshape(9, width)), frequencies,
        w_first, b_first.reshape(1, order), w_second, b_second.reshape(1, order),
        split(w_last), split(rates.reshape(1, width)), split(skip.reshape(1, width)),
        jnp.asarray(forward), jnp.asarray(inverse),
    )
    if not flat:
        out = out.transpose(1, 0, 2).reshape(tokens, width)
    return out


def solution(mesh):
    return jax.shard_map(
        local,
        mesh=mesh,
        in_specs=(
            P(("grp", "seq"), "ch"),
            P(("grp", "seq"), "ch"),
            P(("grp", "seq"), "ch"),
            P(None, None, "ch"),
            P(),
            P(),
            P(),
            P(),
            P(),
            P(None, "ch"),
            P("ch"),
            P("ch"),
        ),
        out_specs=P(("grp", "seq"), "ch"),
        check_vma=False,
    )
```

```python
import functools
import math

import jax
import jax.numpy as jnp
import numpy as np
from jax import lax
from jax.experimental import pallas as pl
from jax.experimental.pallas import tpu as pltpu
from jax.sharding import PartitionSpec as P

HIGH = lax.Precision.HIGHEST
EPS = 1e-06
DECAY_FLOOR = 0.05
LANES = 128
EDGE = 8


def transform_tables(block):
    freq = 2 * np.arange(block)[:, None] + 1
    place = np.arange(2 * block)[None, :]
    angle = 2.0 * np.pi / (4 * block) * (freq * place % (4 * block))
    forward = np.concatenate([np.cos(angle), -np.sin(angle)], axis=0)
    late = angle[:, block:].T
    inverse = np.concatenate([np.cos(late), -np.sin(late)], axis=1) / block
    return forward.astype(np.float32), inverse.astype(np.float32)


def small_sine(x):
    turns = jnp.floor(x * (1.0 / math.pi) + 0.5)
    rest = x - turns * 3.140625
    rest = rest - turns * 9.67502593994140625e-4
    rest = rest - turns * 1.509957990978376432e-7
    odd = (turns.astype(jnp.int32) & 1) == 1
    rest = jnp.where(odd, -rest, rest)
    square = rest * rest
    poly = 2.6083159809786593541503e-06
    poly = poly * square - 0.0001981069071916863322258
    poly = poly * square + 0.00833307858556509017944336
    poly = poly * square - 0.166666597127914428710938
    return rest + rest * (square * poly)


def contract_rows(left, right):
    return lax.dot_general(
        left, right, (((0,), (0,)), ((), ())), precision=HIGH,
        preferred_element_type=jnp.float32,
    )


def kernel(
    parts, flat,
    q_hbm, k_hbm, v_hbm, taps_hbm, freq_ref, w1_hbm, b1_hbm, w2_hbm, b2_hbm,
    w3_hbm, rates_hbm, skip_hbm, fwd_hbm, inv_hbm,
    out_ref,
    q_ref, k_ref, v_ref, taps_ref, w1_ref, b1_ref, w2_ref, b2_ref, w3_ref, rates_ref,
    skip_ref, fwd_ref, inv_ref, load_sems, block_sems,
    tails, send, recv, back, conv, feat, w1x, hid, w2x, filt, gain, spec, prod,
    tail_sems, main_sems, edge_sems, back_sems,
):
    tokens, cw = send.shape[1], send.shape[2]
    length = tokens * parts
    me = lax.axis_index("seq")
    order = sorted(range(1, parts), key=lambda s: (-min(s, parts - s), s))

    def ahead(s):
        return lax.rem(me + s, parts)

    def behind(s):
        return lax.rem(me + parts - s, parts)

    def cols(ref, d, rows=slice(None)):
        if flat:
            return ref[rows, pl.ds(pl.multiple_of(d * cw, LANES), cw)]
        return ref[d, rows, :]

    def part_of(ref, d):
        if flat:
            return ref.at[:, pl.ds(pl.multiple_of(d * cw, LANES), cw)]
        return ref.at[d]

    def taps_of(j, d):
        if flat:
            return taps_ref[j, :, pl.ds(pl.multiple_of(d * cw, LANES), cw)]
        return taps_ref[d, j]

    block_loads = {}
    small = {}

    def load(name, src, dst):
        small[name] = pltpu.make_async_copy(src, dst, load_sems.at[len(small)])
        small[name].start()

    def load_block(j, src, dst, s):
        d = ahead(s)
        block_loads[j, s] = pltpu.make_async_copy(
            part_of(src, d), dst.at[d], block_sems.at[j, s]
        )
        block_loads[j, s].start()

    load("taps", taps_hbm, taps_ref)
    for s in order + [0]:
        load_block(1, k_hbm, k_ref, s)
        load_block(2, v_hbm, v_ref, s)

    def remote(src, dst, sems, s, dest):
        return pltpu.make_async_remote_copy(
            src_ref=src, dst_ref=dst, send_sem=sems.at[0, s], recv_sem=sems.at[1, s],
            device_id={"seq": dest}, device_id_type=pl.DeviceIdType.MESH,
        )

    barrier = pltpu.get_barrier_semaphore()
    for s in order:
        pl.semaphore_signal(
            barrier, inc=1, device_id={"seq": ahead(s)},
            device_id_type=pl.DeviceIdType.MESH,
        )
    pl.semaphore_wait(barrier, parts - 1)

    last = pl.ds(tokens - EDGE, EDGE)
    tail_copies = []
    for j, ref in enumerate((k_hbm, v_hbm, q_hbm)):
        src = ref.at[last, :] if flat else ref.at[:, last, :]
        copy = remote(src, tails.at[j], tail_sems, j, ahead(1))
        copy.start()
        tail_copies.append(copy)
    load("w1", w1_hbm, w1_ref)
    load("b1", b1_hbm, b1_ref)
    load("w2", w2_hbm, w2_ref)
    load("b2", b2_hbm, b2_ref)
    load("w3", part_of(w3_hbm, me), w3_ref)
    load("rates", part_of(rates_hbm, me), rates_ref)
    load("fwd", fwd_hbm, fwd_ref)
    load("inv", inv_hbm, inv_ref)
    load("skip", skip_hbm, skip_ref)
    for s in order + [0]:
        load_block(0, q_hbm, q_ref, s)

    def short(ref, j, d):
        x = ref[d]
        taps = taps_of(j, d)
        return (
            taps[0:1] * x[EDGE:]
            + taps[1:2] * x[EDGE - 1 : tokens - 1]
            + taps[2:3] * x[EDGE - 2 : tokens - 2]
        )

    def short_edge(ref, j, slot, d):
        x = ref[d, 0:EDGE, :]
        before = cols(tails.at[slot], d)
        before = jnp.where(me == 0, jnp.zeros_like(before), before)
        both = jnp.concatenate([before, x], axis=0)
        taps = taps_of(j, d)
        return (
            taps[0:1] * x
            + taps[1:2] * both[EDGE - 1 : 2 * EDGE - 1]
            + taps[2:3] * both[EDGE - 2 : 2 * EDGE - 2]
        )

    main_rows = pl.ds(EDGE, tokens - EDGE)
    edge_rows = pl.ds(0, EDGE)
    main_copies, edge_copies, back_copies = {}, {}, {}
    small["taps"].wait()
    for s in order + [0]:
        d = ahead(s)
        block_loads[1, s].wait()
        block_loads[2, s].wait()
        send[d, EDGE:, :] = short(k_ref, 1, d) * short(v_ref, 2, d)
        if s:
            copy = remote(
                send.at[d, main_rows, :], recv.at[me, main_rows, :], main_sems, s, d
            )
            copy.start()
            main_copies[s] = copy
    for copy in tail_copies:
        copy.wait()
    for s in order + [0]:
        d = ahead(s)
        send[d, :EDGE, :] = short_edge(k_ref, 1, 0, d) * short_edge(v_ref, 2, 1, d)
        if s:
            copy = remote(
                send.at[d, edge_rows, :], recv.at[me, edge_rows, :], edge_sems, s, d
            )
            copy.start()
            edge_copies[s] = copy

    for name in ("w1", "b1", "w2", "b2", "w3", "rates", "fwd", "inv", "skip"):
        small[name].wait()
    width = feat.shape[1]
    bands = freq_ref.shape[0]
    row = lax.broadcasted_iota(jnp.int32, (2 * bands, width), 0)
    position = lax.broadcasted_iota(jnp.int32, (2 * bands, width), 1)
    cycles = jnp.zeros((2 * bands, width), jnp.int32)
    for b in range(bands):
        cycles = jnp.where((row == b) | (row == b + bands), freq_ref[b], cycles)
    quarter = jnp.where(row < bands, length // 4, 0)
    phase = (position * cycles + quarter) & (length - 1)
    feat[...] = jnp.zeros_like(feat)
    feat[0 : 2 * bands, :] = small_sine((2.0 * math.pi / length) * phase.astype(jnp.float32))
    feat[2 * bands : 2 * bands + 1, :] = position[0:1].astype(jnp.float32) / length
    feat[2 * bands + 1 : 2 * bands + 2, :] = jnp.ones((1, width), jnp.float32)
    w1x[...] = jnp.zeros_like(w1x)
    w1x[0 : 2 * bands, :] = w1_ref[1 : 2 * bands + 1, :]
    w1x[2 * bands : 2 * bands + 1, :] = w1_ref[0:1, :]
    w1x[2 * bands + 1 : 2 * bands + 2, :] = b1_ref[...]
    hidden_units = w2_ref.shape[0]
    hid[...] = jnp.zeros_like(hid)
    hid[hidden_units : hidden_units + 1, :] = jnp.ones((1, width), jnp.float32)
    hid[0:hidden_units, :] = small_sine(contract_rows(w1x[...], feat[...]))
    w2x[...] = jnp.zeros_like(w2x)
    w2x[0:hidden_units, :] = w2_ref[...]
    w2x[hidden_units : hidden_units + 1, :] = b2_ref[...]
    hid[0:hidden_units, :] = small_sine(contract_rows(w2x[...], hid[...]))

    filt[0:tokens, :] = jnp.zeros((tokens, cw), jnp.float32)
    w_last = w3_ref[...]
    rates = rates_ref[...]

    def filter_block(j, energy):
        start = pl.multiple_of(j * tokens, tokens)
        raw = contract_rows(hid[0:hidden_units, pl.ds(start, tokens)], w_last)
        n = lax.broadcasted_iota(jnp.int32, (tokens, cw), 0) + j * tokens
        place = n.astype(jnp.float32) / length
        values = raw * (jnp.exp(-place * rates) + DECAY_FLOOR)
        filt[pl.ds(pl.multiple_of(start + tokens, tokens), tokens), :] = values
        return energy + jnp.sum(values * values, axis=0, keepdims=True)

    energy = lax.fori_loop(0, parts, filter_block, jnp.zeros((1, cw), jnp.float32))
    scale = 1.0 / jnp.sqrt(energy + EPS)

    @pl.loop(0, parts)
    def _(j):
        window = filt[pl.ds(pl.multiple_of(j * tokens, tokens), 2 * tokens), :]
        gain[j] = scale * jnp.dot(
            fwd_ref[...], window, precision=HIGH, preferred_element_type=jnp.float32
        )
        prod[j] = jnp.zeros((2 * tokens, cw), jnp.float32)

    def absorb(block, i):
        spec[...] = jnp.dot(
            fwd_ref[:, 0:tokens], block, precision=HIGH, preferred_element_type=jnp.float32
        )

        @pl.loop(0, parts - i)
        def _(j):
            x_re, x_im = spec[0:tokens, :], spec[tokens:, :]
            g_re, g_im = gain[j, 0:tokens, :], gain[j, tokens:, :]
            prod[i + j, 0:tokens, :] += x_re * g_re - x_im * g_im
            prod[i + j, tokens:, :] += x_re * g_im + x_im * g_re

    absorb(send[me], me)
    for s in order:
        main_copies[s].wait_recv()
        edge_copies[s].wait_recv()
        absorb(recv[behind(s)], behind(s))

    def restore(m):
        return jnp.dot(
            inv_ref[...], prod[m], precision=HIGH, preferred_element_type=jnp.float32
        )

    for s in order:
        m = ahead(s)
        conv[m] = restore(m)
        copy = remote(conv.at[m], back.at[me], back_sems, s, m)
        copy.start()
        back_copies[s] = copy
    conv[me] = restore(me)

    def gate(result, d):
        q_short = jnp.concatenate(
            [short_edge(q_ref, 0, 2, d), short(q_ref, 0, d)], axis=0
        )
        value = q_short * (result + cols(skip_ref, d) * send[d])
        if flat:
            out_ref[:, pl.ds(pl.multiple_of(d * cw, LANES), cw)] = value
        else:
            out_ref[d] = value

    for s in order + [0]:
        block_loads[0, s].wait()
    gate(conv[me], me)
    for s in order:
        back_copies[s].wait_recv()
        gate(back[behind(s)], behind(s))
    for s in order:
        main_copies[s].wait_send()
        edge_copies[s].wait_send()
        back_copies[s].wait_send()


def local(
    q_proj, k_proj, v_proj, short_taps, frequencies, w_first, b_first, w_second,
    b_second, w_last, rates, skip,
):
    tokens, width = q_proj.shape
    parts = lax.axis_size("seq")
    cw = width // parts
    flat = cw % LANES == 0
    length = tokens * parts
    order = w_second.shape[0]
    features = w_first.shape[0]

    def split(array):
        if flat:
            return array
        return array.reshape(array.shape[0], parts, cw).transpose(1, 0, 2)

    forward, inverse = transform_tables(tokens)
    tail_shape = (3, EDGE, width) if flat else (3, parts, EDGE, cw)
    out_shape = (tokens, width) if flat else (parts, tokens, cw)
    f32 = jnp.float32
    feature_rows = (features + 1 + 7) // 8 * 8
    blocks = pltpu.VMEM((parts, tokens, cw), f32)
    spectra = pltpu.VMEM((parts, 2 * tokens, cw), f32)
    vmem = pl.BlockSpec(memory_space=pltpu.VMEM)
    hbm = pl.BlockSpec(memory_space=pltpu.HBM)
    smem = pl.BlockSpec(memory_space=pltpu.SMEM)
    sems = pltpu.SemaphoreType.DMA((2, parts))
    taps = short_taps
    if not flat:
        taps = taps.reshape(3, 3, parts, cw).transpose(2, 0, 1, 3)
    out = pl.pallas_call(
        functools.partial(kernel, parts, flat),
        out_shape=jax.ShapeDtypeStruct(out_shape, f32),
        in_specs=[hbm] * 4 + [smem] + [hbm] * 9,
        out_specs=vmem,
        scratch_shapes=[
            blocks, blocks, blocks,
            pltpu.VMEM(taps.shape, f32),
            pltpu.VMEM((features, order), f32),
            pltpu.VMEM((1, order), f32),
            pltpu.VMEM((order, order), f32),
            pltpu.VMEM((1, order), f32),
            pltpu.VMEM((order, cw), f32),
            pltpu.VMEM((1, cw), f32),
            pltpu.VMEM((1, width) if flat else (parts, 1, cw), f32),
            pltpu.VMEM((2 * tokens, 2 * tokens), f32),
            pltpu.VMEM((tokens, 2 * tokens), f32),
            pltpu.SemaphoreType.DMA((10,)),
            pltpu.SemaphoreType.DMA((3, parts)),
            pltpu.VMEM(tail_shape, f32),
            blocks, blocks, blocks, blocks,
            pltpu.VMEM((feature_rows, length), f32),
            pltpu.VMEM((feature_rows, order), f32),
            pltpu.VMEM((order + 8, length), f32),
            pltpu.VMEM((order + 8, order), f32),
            pltpu.VMEM((length + tokens, cw), f32),
            spectra,
            pltpu.VMEM((2 * tokens, cw), f32),
            spectra,
            pltpu.SemaphoreType.DMA((2, 3)),
            sems, sems, sems,
        ],
        compiler_params=pltpu.CompilerParams(
            collective_id=0, has_side_effects=True, vmem_limit_bytes=62 * 1024 * 1024
        ),
        cost_estimate=pl.CostEstimate(
            flops=6 * length * tokens * cw * 8, bytes_accessed=16 * tokens * width,
            transcendentals=length * cw,
        ),
    )(
        split(q_proj), split(k_proj), split(v_proj),
        taps, frequencies,
        w_first, b_first.reshape(1, order), w_second, b_second.reshape(1, order),
        split(w_last), split(rates.reshape(1, width)), split(skip.reshape(1, width)),
        jnp.asarray(forward), jnp.asarray(inverse),
    )
    if not flat:
        out = out.transpose(1, 0, 2).reshape(tokens, width)
    return out


def solution(mesh):
    return jax.shard_map(
        local,
        mesh=mesh,
        in_specs=(
            P(("grp", "seq"), "ch"),
            P(("grp", "seq"), "ch"),
            P(("grp", "seq"), "ch"),
            P(None, None, "ch"),
            P(),
            P(),
            P(),
            P(),
            P(),
            P(None, "ch"),
            P("ch"),
            P("ch"),
        ),
        out_specs=P(("grp", "seq"), "ch"),
        check_vma=False,
    )
```

```python
import functools
import math

import jax
import jax.numpy as jnp
import numpy as np
from jax import lax
from jax.experimental import pallas as pl
from jax.experimental.pallas import tpu as pltpu
from jax.sharding import PartitionSpec as P

HIGH = lax.Precision.HIGHEST
EPS = 1e-06
DECAY_FLOOR = 0.05
LANES = 128
EDGE = 8


def transform_tables(block):
    freq = 2 * np.arange(block)[:, None] + 1
    place = np.arange(2 * block)[None, :]
    angle = 2.0 * np.pi / (4 * block) * (freq * place % (4 * block))
    forward = np.concatenate([np.cos(angle), -np.sin(angle)], axis=0)
    late = angle[:, block:].T
    inverse = np.concatenate([np.cos(late), -np.sin(late)], axis=1) / block
    return forward.astype(np.float32), inverse.astype(np.float32)


def small_sine(x):
    turns = jnp.floor(x * (1.0 / math.pi) + 0.5)
    rest = x - turns * 3.140625
    rest = rest - turns * 9.67502593994140625e-4
    rest = rest - turns * 1.509957990978376432e-7
    odd = (turns.astype(jnp.int32) & 1) == 1
    rest = jnp.where(odd, -rest, rest)
    square = rest * rest
    poly = 2.6083159809786593541503e-06
    poly = poly * square - 0.0001981069071916863322258
    poly = poly * square + 0.00833307858556509017944336
    poly = poly * square - 0.166666597127914428710938
    return rest + rest * (square * poly)


def contract_rows(left, right):
    return lax.dot_general(
        left, right, (((0,), (0,)), ((), ())), precision=HIGH,
        preferred_element_type=jnp.float32,
    )


def kernel(
    parts, flat,
    q_hbm, k_hbm, v_hbm, taps_hbm, freq_ref, w1_hbm, b1_hbm, w2_hbm, b2_hbm,
    w3_hbm, rates_hbm, skip_hbm, fwd_hbm, inv_hbm,
    out_ref,
    q_ref, k_ref, v_ref, taps_ref, w1_ref, b1_ref, w2_ref, b2_ref, w3_ref, rates_ref,
    skip_ref, fwd_ref, inv_ref, load_sems, block_sems,
    tails, send, recv, back, conv, feat, w1x, hid, w2x, filt, gain, spec, prod,
    tail_sems, main_sems, edge_sems, back_sems,
):
    tokens, cw = send.shape[1], send.shape[2]
    length = tokens * parts
    me = lax.axis_index("seq")
    half = parts // 2

    def turn(t):
        return half + (1 - 2 * (t % 2)) * ((t + 1) // 2)

    def ahead(s):
        return lax.rem(me + s, parts)

    def behind(s):
        return lax.rem(me + parts - s, parts)

    def cols(ref, d, rows=slice(None)):
        if flat:
            return ref[rows, pl.ds(pl.multiple_of(d * cw, LANES), cw)]
        return ref[d, rows, :]

    def part_of(ref, d):
        if flat:
            return ref.at[:, pl.ds(pl.multiple_of(d * cw, LANES), cw)]
        return ref.at[d]

    def taps_of(j, d):
        if flat:
            return taps_ref[j, :, pl.ds(pl.multiple_of(d * cw, LANES), cw)]
        return taps_ref[d, j]

    barrier = pltpu.get_barrier_semaphore()

    @pl.loop(1, parts)
    def _(s):
        pl.semaphore_signal(
            barrier, inc=1, device_id={"seq": ahead(s)},
            device_id_type=pl.DeviceIdType.MESH,
        )

    small = {}

    def load(name, src, dst):
        small[name] = pltpu.make_async_copy(src, dst, load_sems.at[len(small)])
        small[name].start()

    def block_load(j, src, dst, s):
        d = ahead(s)
        return pltpu.make_async_copy(part_of(src, d), dst.at[d], block_sems.at[j, s])

    load("taps", taps_hbm, taps_ref)

    @pl.loop(0, parts)
    def _(t):
        block_load(1, k_hbm, k_ref, turn(t)).start()
        block_load(2, v_hbm, v_ref, turn(t)).start()

    def remote(src, dst, sems, s, dest):
        return pltpu.make_async_remote_copy(
            src_ref=src, dst_ref=dst, send_sem=sems.at[0, s], recv_sem=sems.at[1, s],
            device_id={"seq": dest}, device_id_type=pl.DeviceIdType.MESH,
        )


    load("w1", w1_hbm, w1_ref)
    load("b1", b1_hbm, b1_ref)
    load("w2", w2_hbm, w2_ref)
    load("b2", b2_hbm, b2_ref)
    load("w3", part_of(w3_hbm, me), w3_ref)
    load("rates", part_of(rates_hbm, me), rates_ref)
    load("fwd", fwd_hbm, fwd_ref)
    load("inv", inv_hbm, inv_ref)
    load("skip", skip_hbm, skip_ref)

    @pl.loop(0, parts)
    def _(t):
        block_load(0, q_hbm, q_ref, turn(t)).start()

    def short(ref, j, d):
        x = ref[d]
        taps = taps_of(j, d)
        return (
            taps[0:1] * x[EDGE:]
            + taps[1:2] * x[EDGE - 1 : tokens - 1]
            + taps[2:3] * x[EDGE - 2 : tokens - 2]
        )

    def short_edge(ref, j, slot, d):
        x = ref[d, 0:EDGE, :]
        before = cols(tails.at[slot], d)
        before = jnp.where(me == 0, jnp.zeros_like(before), before)
        both = jnp.concatenate([before, x], axis=0)
        taps = taps_of(j, d)
        return (
            taps[0:1] * x
            + taps[1:2] * both[EDGE - 1 : 2 * EDGE - 1]
            + taps[2:3] * both[EDGE - 2 : 2 * EDGE - 2]
        )

    main_rows = pl.ds(EDGE, tokens - EDGE)
    edge_rows = pl.ds(0, EDGE)
    def main_copy(s):
        d = ahead(s)
        return remote(
            send.at[d, main_rows, :], recv.at[me, main_rows, :], main_sems, s, d
        )

    def edge_copy(s):
        d = ahead(s)
        return remote(
            send.at[d, edge_rows, :], recv.at[me, edge_rows, :], edge_sems, s, d
        )

    def back_copy(s):
        m = ahead(s)
        return remote(conv.at[m], back.at[me], back_sems, s, m)

    small["taps"].wait()

    def mix_main(s):
        d = ahead(s)
        block_load(1, k_hbm, k_ref, s).wait()
        block_load(2, v_hbm, v_ref, s).wait()
        send[d, EDGE:, :] = short(k_ref, 1, d) * short(v_ref, 2, d)

    def mix_edge(s):
        d = ahead(s)
        send[d, :EDGE, :] = short_edge(k_ref, 1, 0, d) * short_edge(v_ref, 2, 1, d)

    @pl.loop(0, parts)
    def _(t):
        mix_main(turn(t))

    pl.semaphore_wait(barrier, parts - 1)

    last = pl.ds(tokens - EDGE, EDGE)
    tail_copies = []
    for j, ref in enumerate((k_hbm, v_hbm, q_hbm)):
        src = ref.at[last, :] if flat else ref.at[:, last, :]
        copy = remote(src, tails.at[j], tail_sems, j, ahead(1))
        copy.start()
        tail_copies.append(copy)
    @pl.loop(0, parts - 1)
    def _(t):
        main_copy(turn(t)).start()

    for copy in tail_copies:
        copy.wait()

    @pl.loop(0, parts)
    def _(t):
        s = turn(t)
        mix_edge(s)

        @pl.when(t < parts - 1)
        def _():
            edge_copy(s).start()

    for name in ("w1", "b1", "w2", "b2", "w3", "rates", "fwd", "inv", "skip"):
        small[name].wait()
    width = feat.shape[1]
    bands = freq_ref.shape[0]
    row = lax.broadcasted_iota(jnp.int32, (2 * bands, width), 0)
    position = lax.broadcasted_iota(jnp.int32, (2 * bands, width), 1)
    cycles = jnp.zeros((2 * bands, width), jnp.int32)
    for b in range(bands):
        cycles = jnp.where((row == b) | (row == b + bands), freq_ref[b], cycles)
    quarter = jnp.where(row < bands, length // 4, 0)
    phase = (position * cycles + quarter) & (length - 1)
    feat[...] = jnp.zeros_like(feat)
    feat[0 : 2 * bands, :] = small_sine((2.0 * math.pi / length) * phase.astype(jnp.float32))
    feat[2 * bands : 2 * bands + 1, :] = position[0:1].astype(jnp.float32) / length
    feat[2 * bands + 1 : 2 * bands + 2, :] = jnp.ones((1, width), jnp.float32)
    w1x[...] = jnp.zeros_like(w1x)
    w1x[0 : 2 * bands, :] = w1_ref[1 : 2 * bands + 1, :]
    w1x[2 * bands : 2 * bands + 1, :] = w1_ref[0:1, :]
    w1x[2 * bands + 1 : 2 * bands + 2, :] = b1_ref[...]
    hidden_units = w2_ref.shape[0]
    hid[...] = jnp.zeros_like(hid)
    hid[hidden_units : hidden_units + 1, :] = jnp.ones((1, width), jnp.float32)
    hid[0:hidden_units, :] = small_sine(contract_rows(w1x[...], feat[...]))
    w2x[...] = jnp.zeros_like(w2x)
    w2x[0:hidden_units, :] = w2_ref[...]
    w2x[hidden_units : hidden_units + 1, :] = b2_ref[...]
    hid[0:hidden_units, :] = small_sine(contract_rows(w2x[...], hid[...]))

    filt[0:tokens, :] = jnp.zeros((tokens, cw), jnp.float32)
    w_last = w3_ref[...]
    rates = rates_ref[...]

    def filter_block(j, energy):
        start = pl.multiple_of(j * tokens, tokens)
        raw = contract_rows(hid[0:hidden_units, pl.ds(start, tokens)], w_last)
        n = lax.broadcasted_iota(jnp.int32, (tokens, cw), 0) + j * tokens
        place = n.astype(jnp.float32) / length
        values = raw * (jnp.exp(-place * rates) + DECAY_FLOOR)
        filt[pl.ds(pl.multiple_of(start + tokens, tokens), tokens), :] = values
        return energy + jnp.sum(values * values, axis=0, keepdims=True)

    energy = lax.fori_loop(0, parts, filter_block, jnp.zeros((1, cw), jnp.float32))
    scale = 1.0 / jnp.sqrt(energy + EPS)

    @pl.loop(0, parts)
    def _(j):
        window = filt[pl.ds(pl.multiple_of(j * tokens, tokens), 2 * tokens), :]
        gain[j] = scale * jnp.dot(
            fwd_ref[...], window, precision=HIGH, preferred_element_type=jnp.float32
        )
        prod[j] = jnp.zeros((2 * tokens, cw), jnp.float32)

    def absorb(block, i):
        spec[...] = jnp.dot(
            fwd_ref[:, 0:tokens], block, precision=HIGH, preferred_element_type=jnp.float32
        )

        @pl.loop(0, parts - i)
        def _(j):
            x_re, x_im = spec[0:tokens, :], spec[tokens:, :]
            g_re, g_im = gain[j, 0:tokens, :], gain[j, tokens:, :]
            prod[i + j, 0:tokens, :] += x_re * g_re - x_im * g_im
            prod[i + j, tokens:, :] += x_re * g_im + x_im * g_re

    absorb(send[me], me)

    @pl.loop(0, parts - 1)
    def _(t):
        s = turn(t)
        main_copy(s).wait_recv()
        edge_copy(s).wait_recv()
        absorb(recv[behind(s)], behind(s))

    def restore(m):
        return jnp.dot(
            inv_ref[...], prod[m], precision=HIGH, preferred_element_type=jnp.float32
        )

    @pl.loop(0, parts)
    def _(t):
        s = turn(t)
        conv[ahead(s)] = restore(ahead(s))

        @pl.when(t < parts - 1)
        def _():
            back_copy(s).start()

    def gate(result, d):
        q_short = jnp.concatenate(
            [short_edge(q_ref, 0, 2, d), short(q_ref, 0, d)], axis=0
        )
        value = q_short * (result + cols(skip_ref, d) * send[d])
        if flat:
            out_ref[:, pl.ds(pl.multiple_of(d * cw, LANES), cw)] = value
        else:
            out_ref[d] = value

    @pl.loop(0, parts)
    def _(t):
        block_load(0, q_hbm, q_ref, turn(t)).wait()

    gate(conv[me], me)

    @pl.loop(0, parts - 1)
    def _(t):
        s = turn(t)
        back_copy(s).wait_recv()
        gate(back[behind(s)], behind(s))

    @pl.loop(0, parts - 1)
    def _(t):
        s = turn(t)
        main_copy(s).wait_send()
        edge_copy(s).wait_send()
        back_copy(s).wait_send()


def local(
    q_proj, k_proj, v_proj, short_taps, frequencies, w_first, b_first, w_second,
    b_second, w_last, rates, skip,
):
    tokens, width = q_proj.shape
    parts = lax.axis_size("seq")
    cw = width // parts
    flat = cw % LANES == 0
    length = tokens * parts
    order = w_second.shape[0]
    features = w_first.shape[0]

    def split(array):
        if flat:
            return array
        return array.reshape(array.shape[0], parts, cw).transpose(1, 0, 2)

    forward, inverse = transform_tables(tokens)
    tail_shape = (3, EDGE, width) if flat else (3, parts, EDGE, cw)
    out_shape = (tokens, width) if flat else (parts, tokens, cw)
    f32 = jnp.float32
    feature_rows = (features + 1 + 7) // 8 * 8
    blocks = pltpu.VMEM((parts, tokens, cw), f32)
    spectra = pltpu.VMEM((parts, 2 * tokens, cw), f32)
    vmem = pl.BlockSpec(memory_space=pltpu.VMEM)
    hbm = pl.BlockSpec(memory_space=pltpu.HBM)
    smem = pl.BlockSpec(memory_space=pltpu.SMEM)
    sems = pltpu.SemaphoreType.DMA((2, parts))
    taps = short_taps
    if not flat:
        taps = taps.reshape(3, 3, parts, cw).transpose(2, 0, 1, 3)
    out = pl.pallas_call(
        functools.partial(kernel, parts, flat),
        out_shape=jax.ShapeDtypeStruct(out_shape, f32),
        in_specs=[hbm] * 4 + [smem] + [hbm] * 9,
        out_specs=vmem,
        scratch_shapes=[
            blocks, blocks, blocks,
            pltpu.VMEM(taps.shape, f32),
            pltpu.VMEM((features, order), f32),
            pltpu.VMEM((1, order), f32),
            pltpu.VMEM((order, order), f32),
            pltpu.VMEM((1, order), f32),
            pltpu.VMEM((order, cw), f32),
            pltpu.VMEM((1, cw), f32),
            pltpu.VMEM((1, width) if flat else (parts, 1, cw), f32),
            pltpu.VMEM((2 * tokens, 2 * tokens), f32),
            pltpu.VMEM((tokens, 2 * tokens), f32),
            pltpu.SemaphoreType.DMA((10,)),
            pltpu.SemaphoreType.DMA((3, parts)),
            pltpu.VMEM(tail_shape, f32),
            blocks, blocks, blocks, blocks,
            pltpu.VMEM((feature_rows, length), f32),
            pltpu.VMEM((feature_rows, order), f32),
            pltpu.VMEM((order + 8, length), f32),
            pltpu.VMEM((order + 8, order), f32),
            pltpu.VMEM((length + tokens, cw), f32),
            spectra,
            pltpu.VMEM((2 * tokens, cw), f32),
            spectra,
            pltpu.SemaphoreType.DMA((2, 3)),
            sems, sems, sems,
        ],
        compiler_params=pltpu.CompilerParams(
            collective_id=0, has_side_effects=True, vmem_limit_bytes=59 * 1024 * 1024
        ),
        cost_estimate=pl.CostEstimate(
            flops=6 * length * tokens * cw * 8, bytes_accessed=16 * tokens * width,
            transcendentals=length * cw,
        ),
    )(
        split(q_proj), split(k_proj), split(v_proj),
        taps, frequencies,
        w_first, b_first.reshape(1, order), w_second, b_second.reshape(1, order),
        split(w_last), split(rates.reshape(1, width)), split(skip.reshape(1, width)),
        jnp.asarray(forward), jnp.asarray(inverse),
    )
    if not flat:
        out = out.transpose(1, 0, 2).reshape(tokens, width)
    return out


def solution(mesh):
    return jax.shard_map(
        local,
        mesh=mesh,
        in_specs=(
            P(("grp", "seq"), "ch"),
            P(("grp", "seq"), "ch"),
            P(("grp", "seq"), "ch"),
            P(None, None, "ch"),
            P(),
            P(),
            P(),
            P(),
            P(),
            P(None, "ch"),
            P("ch"),
            P("ch"),
        ),
        out_specs=P(("grp", "seq"), "ch"),
        check_vma=False,
    )
```

```python
import functools
import math

import jax
import jax.numpy as jnp
import numpy as np
from jax import lax
from jax.experimental import pallas as pl
from jax.experimental.pallas import tpu as pltpu
from jax.sharding import PartitionSpec as P

HIGH = lax.Precision.HIGHEST
EPS = 1e-06
DECAY_FLOOR = 0.05
LANES = 128
EDGE = 8


def transform_tables(block):
    freq = 2 * np.arange(block)[:, None] + 1
    place = np.arange(2 * block)[None, :]
    angle = 2.0 * np.pi / (4 * block) * (freq * place % (4 * block))
    forward = np.concatenate([np.cos(angle), -np.sin(angle)], axis=0)
    late = angle[:, block:].T
    inverse = np.concatenate([np.cos(late), -np.sin(late)], axis=1) / block
    return forward.astype(np.float32), inverse.astype(np.float32)


def small_sine(x):
    turns = jnp.floor(x * (1.0 / math.pi) + 0.5)
    rest = x - turns * 3.140625
    rest = rest - turns * 9.67502593994140625e-4
    rest = rest - turns * 1.509957990978376432e-7
    odd = (turns.astype(jnp.int32) & 1) == 1
    rest = jnp.where(odd, -rest, rest)
    square = rest * rest
    poly = 2.6083159809786593541503e-06
    poly = poly * square - 0.0001981069071916863322258
    poly = poly * square + 0.00833307858556509017944336
    poly = poly * square - 0.166666597127914428710938
    return rest + rest * (square * poly)


def contract_rows(left, right):
    return lax.dot_general(
        left, right, (((0,), (0,)), ((), ())), precision=HIGH,
        preferred_element_type=jnp.float32,
    )


def kernel(
    parts, flat,
    q_hbm, k_hbm, v_hbm, taps_hbm, freq_ref, w1_hbm, b1_hbm, w2_hbm, b2_hbm,
    w3_hbm, rates_hbm, skip_hbm, fwd_hbm, inv_hbm,
    out_ref,
    q_ref, k_ref, v_ref, taps_ref, w1_ref, b1_ref, w2_ref, b2_ref, w3_ref, rates_ref,
    skip_ref, fwd_ref, inv_ref, load_sems, block_sems,
    tails, send, recv, back, conv, feat, w1x, hid, w2x, filt, gain, spec, prod,
    tail_sems, main_sems, edge_sems, back_sems,
):
    tokens, cw = send.shape[1], send.shape[2]
    length = tokens * parts
    me = lax.axis_index("seq")
    half = parts // 2

    def turn(t):
        return half + (1 - 2 * (t % 2)) * ((t + 1) // 2)

    def ahead(s):
        return lax.rem(me + s, parts)

    def behind(s):
        return lax.rem(me + parts - s, parts)

    def cols(ref, d, rows=slice(None)):
        if flat:
            return ref[rows, pl.ds(pl.multiple_of(d * cw, LANES), cw)]
        return ref[d, rows, :]

    def part_of(ref, d):
        if flat:
            return ref.at[:, pl.ds(pl.multiple_of(d * cw, LANES), cw)]
        return ref.at[d]

    def taps_of(j, d):
        if flat:
            return taps_ref[j, :, pl.ds(pl.multiple_of(d * cw, LANES), cw)]
        return taps_ref[d, j]

    barrier = pltpu.get_barrier_semaphore()

    @pl.loop(1, parts)
    def _(s):
        pl.semaphore_signal(
            barrier, inc=1, device_id={"seq": ahead(s)},
            device_id_type=pl.DeviceIdType.MESH,
        )

    small = {}

    def load(name, src, dst):
        small[name] = pltpu.make_async_copy(src, dst, load_sems.at[len(small)])
        small[name].start()

    def block_load(j, src, dst, s):
        d = ahead(s)
        return pltpu.make_async_copy(part_of(src, d), dst.at[d], block_sems.at[j, s])

    load("taps", taps_hbm, taps_ref)

    @pl.loop(0, parts)
    def _(t):
        block_load(1, k_hbm, k_ref, turn(t)).start()
        block_load(2, v_hbm, v_ref, turn(t)).start()

    def remote(src, dst, sems, s, dest):
        return pltpu.make_async_remote_copy(
            src_ref=src, dst_ref=dst, send_sem=sems.at[0, s], recv_sem=sems.at[1, s],
            device_id={"seq": dest}, device_id_type=pl.DeviceIdType.MESH,
        )


    load("w1", w1_hbm, w1_ref)
    load("b1", b1_hbm, b1_ref)
    load("w2", w2_hbm, w2_ref)
    load("b2", b2_hbm, b2_ref)
    load("w3", part_of(w3_hbm, me), w3_ref)
    load("rates", part_of(rates_hbm, me), rates_ref)
    load("fwd", fwd_hbm, fwd_ref)
    load("inv", inv_hbm, inv_ref)
    load("skip", skip_hbm, skip_ref)

    @pl.loop(0, parts)
    def _(t):
        block_load(0, q_hbm, q_ref, turn(t)).start()

    def short(ref, j, d):
        x = ref[d]
        taps = taps_of(j, d)
        return (
            taps[0:1] * x[EDGE:]
            + taps[1:2] * x[EDGE - 1 : tokens - 1]
            + taps[2:3] * x[EDGE - 2 : tokens - 2]
        )

    def short_edge(ref, j, slot, d):
        x = ref[d, 0:EDGE, :]
        before = cols(tails.at[slot], d)
        before = jnp.where(me == 0, jnp.zeros_like(before), before)
        both = jnp.concatenate([before, x], axis=0)
        taps = taps_of(j, d)
        return (
            taps[0:1] * x
            + taps[1:2] * both[EDGE - 1 : 2 * EDGE - 1]
            + taps[2:3] * both[EDGE - 2 : 2 * EDGE - 2]
        )

    main_rows = pl.ds(EDGE, tokens - EDGE)
    edge_rows = pl.ds(0, EDGE)
    def main_copy(s):
        d = ahead(s)
        return remote(
            send.at[d, main_rows, :], recv.at[me, main_rows, :], main_sems, s, d
        )

    def edge_copy(s):
        d = ahead(s)
        return remote(
            send.at[d, edge_rows, :], recv.at[me, edge_rows, :], edge_sems, s, d
        )

    def back_copy(s):
        m = ahead(s)
        return remote(conv.at[m], back.at[me], back_sems, s, m)

    small["taps"].wait()

    def mix_main(s):
        d = ahead(s)
        block_load(1, k_hbm, k_ref, s).wait()
        block_load(2, v_hbm, v_ref, s).wait()
        send[d, EDGE:, :] = short(k_ref, 1, d) * short(v_ref, 2, d)

    def mix_edge(s):
        d = ahead(s)
        send[d, :EDGE, :] = short_edge(k_ref, 1, 0, d) * short_edge(v_ref, 2, 1, d)

    @pl.loop(0, parts)
    def _(t):
        mix_main(turn(t))

    pl.semaphore_wait(barrier, parts - 1)

    last = pl.ds(tokens - EDGE, EDGE)
    tail_copies = []
    for j, ref in enumerate((k_hbm, v_hbm, q_hbm)):
        src = ref.at[last, :] if flat else ref.at[:, last, :]
        copy = remote(src, tails.at[j], tail_sems, j, ahead(1))
        copy.start()
        tail_copies.append(copy)
    @pl.loop(0, parts - 1)
    def _(t):
        main_copy(turn(t)).start()

    for copy in tail_copies:
        copy.wait()

    @pl.loop(0, parts)
    def _(t):
        s = turn(t)
        mix_edge(s)

        @pl.when(t < parts - 1)
        def _():
            edge_copy(s).start()

    for name in ("w1", "b1", "w2", "b2", "w3", "rates", "fwd", "inv", "skip"):
        small[name].wait()
    width = feat.shape[1]
    bands = freq_ref.shape[0]
    row = lax.broadcasted_iota(jnp.int32, (2 * bands, width), 0)
    position = lax.broadcasted_iota(jnp.int32, (2 * bands, width), 1)
    cycles = jnp.zeros((2 * bands, width), jnp.int32)
    for b in range(bands):
        cycles = jnp.where((row == b) | (row == b + bands), freq_ref[b], cycles)
    quarter = jnp.where(row < bands, length // 4, 0)
    phase = (position * cycles + quarter) & (length - 1)
    feat[...] = jnp.zeros_like(feat)
    feat[0 : 2 * bands, :] = small_sine((2.0 * math.pi / length) * phase.astype(jnp.float32))
    feat[2 * bands : 2 * bands + 1, :] = position[0:1].astype(jnp.float32) / length
    feat[2 * bands + 1 : 2 * bands + 2, :] = jnp.ones((1, width), jnp.float32)
    w1x[...] = jnp.zeros_like(w1x)
    w1x[0 : 2 * bands, :] = w1_ref[1 : 2 * bands + 1, :]
    w1x[2 * bands : 2 * bands + 1, :] = w1_ref[0:1, :]
    w1x[2 * bands + 1 : 2 * bands + 2, :] = b1_ref[...]
    hidden_units = w2_ref.shape[0]
    hid[...] = jnp.zeros_like(hid)
    hid[hidden_units : hidden_units + 1, :] = jnp.ones((1, width), jnp.float32)
    hid[0:hidden_units, :] = small_sine(contract_rows(w1x[...], feat[...]))
    w2x[...] = jnp.zeros_like(w2x)
    w2x[0:hidden_units, :] = w2_ref[...]
    w2x[hidden_units : hidden_units + 1, :] = b2_ref[...]
    hid[0:hidden_units, :] = small_sine(contract_rows(w2x[...], hid[...]))

    filt[0:tokens, :] = jnp.zeros((tokens, cw), jnp.float32)
    w_last = w3_ref[...]
    rates = rates_ref[...]

    def filter_block(j, energy):
        start = pl.multiple_of(j * tokens, tokens)
        raw = contract_rows(hid[0:hidden_units, pl.ds(start, tokens)], w_last)
        n = lax.broadcasted_iota(jnp.int32, (tokens, cw), 0) + j * tokens
        place = n.astype(jnp.float32) / length
        values = raw * (jnp.exp(-place * rates) + DECAY_FLOOR)
        filt[pl.ds(pl.multiple_of(start + tokens, tokens), tokens), :] = values
        return energy + jnp.sum(values * values, axis=0, keepdims=True)

    energy = lax.fori_loop(0, parts, filter_block, jnp.zeros((1, cw), jnp.float32))
    scale = 1.0 / jnp.sqrt(energy + EPS)

    @pl.loop(0, parts)
    def _(j):
        window = filt[pl.ds(pl.multiple_of(j * tokens, tokens), 2 * tokens), :]
        gain[j] = scale * jnp.dot(
            fwd_ref[...], window, precision=HIGH, preferred_element_type=jnp.float32
        )
        prod[j] = jnp.zeros((2 * tokens, cw), jnp.float32)

    def absorb(block, i):
        spec[...] = jnp.dot(
            fwd_ref[:, 0:tokens], block, precision=lax.Precision.HIGH, preferred_element_type=jnp.float32
        )

        @pl.loop(0, parts - i)
        def _(j):
            x_re, x_im = spec[0:tokens, :], spec[tokens:, :]
            g_re, g_im = gain[j, 0:tokens, :], gain[j, tokens:, :]
            prod[i + j, 0:tokens, :] += x_re * g_re - x_im * g_im
            prod[i + j, tokens:, :] += x_re * g_im + x_im * g_re

    absorb(send[me], me)

    @pl.loop(0, parts - 1)
    def _(t):
        s = turn(t)
        main_copy(s).wait_recv()
        edge_copy(s).wait_recv()
        absorb(recv[behind(s)], behind(s))

    def restore(m):
        return jnp.dot(
            inv_ref[...], prod[m], precision=lax.Precision.HIGH, preferred_element_type=jnp.float32
        )

    @pl.loop(0, parts)
    def _(t):
        s = turn(t)
        conv[ahead(s)] = restore(ahead(s))

        @pl.when(t < parts - 1)
        def _():
            back_copy(s).start()

    def gate(result, d):
        q_short = jnp.concatenate(
            [short_edge(q_ref, 0, 2, d), short(q_ref, 0, d)], axis=0
        )
        value = q_short * (result + cols(skip_ref, d) * send[d])
        if flat:
            out_ref[:, pl.ds(pl.multiple_of(d * cw, LANES), cw)] = value
        else:
            out_ref[d] = value

    @pl.loop(0, parts)
    def _(t):
        block_load(0, q_hbm, q_ref, turn(t)).wait()

    gate(conv[me], me)

    @pl.loop(0, parts - 1)
    def _(t):
        s = turn(t)
        back_copy(s).wait_recv()
        gate(back[behind(s)], behind(s))

    @pl.loop(0, parts - 1)
    def _(t):
        s = turn(t)
        main_copy(s).wait_send()
        edge_copy(s).wait_send()
        back_copy(s).wait_send()


def local(
    q_proj, k_proj, v_proj, short_taps, frequencies, w_first, b_first, w_second,
    b_second, w_last, rates, skip,
):
    tokens, width = q_proj.shape
    parts = lax.axis_size("seq")
    cw = width // parts
    flat = cw % LANES == 0
    length = tokens * parts
    order = w_second.shape[0]
    features = w_first.shape[0]

    def split(array):
        if flat:
            return array
        return array.reshape(array.shape[0], parts, cw).transpose(1, 0, 2)

    forward, inverse = transform_tables(tokens)
    tail_shape = (3, EDGE, width) if flat else (3, parts, EDGE, cw)
    out_shape = (tokens, width) if flat else (parts, tokens, cw)
    f32 = jnp.float32
    feature_rows = (features + 1 + 7) // 8 * 8
    blocks = pltpu.VMEM((parts, tokens, cw), f32)
    spectra = pltpu.VMEM((parts, 2 * tokens, cw), f32)
    vmem = pl.BlockSpec(memory_space=pltpu.VMEM)
    hbm = pl.BlockSpec(memory_space=pltpu.HBM)
    smem = pl.BlockSpec(memory_space=pltpu.SMEM)
    sems = pltpu.SemaphoreType.DMA((2, parts))
    taps = short_taps
    if not flat:
        taps = taps.reshape(3, 3, parts, cw).transpose(2, 0, 1, 3)
    out = pl.pallas_call(
        functools.partial(kernel, parts, flat),
        out_shape=jax.ShapeDtypeStruct(out_shape, f32),
        in_specs=[hbm] * 4 + [smem] + [hbm] * 9,
        out_specs=vmem,
        scratch_shapes=[
            blocks, blocks, blocks,
            pltpu.VMEM(taps.shape, f32),
            pltpu.VMEM((features, order), f32),
            pltpu.VMEM((1, order), f32),
            pltpu.VMEM((order, order), f32),
            pltpu.VMEM((1, order), f32),
            pltpu.VMEM((order, cw), f32),
            pltpu.VMEM((1, cw), f32),
            pltpu.VMEM((1, width) if flat else (parts, 1, cw), f32),
            pltpu.VMEM((2 * tokens, 2 * tokens), f32),
            pltpu.VMEM((tokens, 2 * tokens), f32),
            pltpu.SemaphoreType.DMA((10,)),
            pltpu.SemaphoreType.DMA((3, parts)),
            pltpu.VMEM(tail_shape, f32),
            blocks, blocks, blocks, blocks,
            pltpu.VMEM((feature_rows, length), f32),
            pltpu.VMEM((feature_rows, order), f32),
            pltpu.VMEM((order + 8, length), f32),
            pltpu.VMEM((order + 8, order), f32),
            pltpu.VMEM((length + tokens, cw), f32),
            spectra,
            pltpu.VMEM((2 * tokens, cw), f32),
            spectra,
            pltpu.SemaphoreType.DMA((2, 3)),
            sems, sems, sems,
        ],
        compiler_params=pltpu.CompilerParams(
            collective_id=0, has_side_effects=True, vmem_limit_bytes=59 * 1024 * 1024
        ),
        cost_estimate=pl.CostEstimate(
            flops=6 * length * tokens * cw * 8, bytes_accessed=16 * tokens * width,
            transcendentals=length * cw,
        ),
    )(
        split(q_proj), split(k_proj), split(v_proj),
        taps, frequencies,
        w_first, b_first.reshape(1, order), w_second, b_second.reshape(1, order),
        split(w_last), split(rates.reshape(1, width)), split(skip.reshape(1, width)),
        jnp.asarray(forward), jnp.asarray(inverse),
    )
    if not flat:
        out = out.transpose(1, 0, 2).reshape(tokens, width)
    return out


def solution(mesh):
    return jax.shard_map(
        local,
        mesh=mesh,
        in_specs=(
            P(("grp", "seq"), "ch"),
            P(("grp", "seq"), "ch"),
            P(("grp", "seq"), "ch"),
            P(None, None, "ch"),
            P(),
            P(),
            P(),
            P(),
            P(),
            P(None, "ch"),
            P("ch"),
            P("ch"),
        ),
        out_specs=P(("grp", "seq"), "ch"),
        check_vma=False,
    )
```
